512 devices in a mesh: date: 32 (over y_lo, z), row: 16 (over x, y_hi, core).
Axes of the slice: x: 4, y: 4 (y_hi: 2, y_lo: 2; y = y_hi * 2 + y_lo), z: 16, core: 2. Of those that a mesh axis runs over, the one named last changes fastest.
Arguments:
- slc: bfloat16 [2, 128, 256, 1024], P(None, 'date', 'row'), may hold values from -64 to 64
Outputs:
- coherence: float32 [2, 128, 128, 32, 128], P(None, 'date', None, 'row')
The draws below stay inside these ranges and needn't reach their ends.
All inputs are finite; a program needn't handle non-finite values.
Results may differ from the reference program's by a relative error of at most 0.0013.
Values may be sent and summed in bfloat16 or wider, within the bound.
No kernel may reach another device: no remote copies, remote signals or barrier semaphores. Data moves between devices by JAX's collectives and lax.ppermute only.
A program may use at most 64 MiB of HBM per device.

```python
import math
import jax
import jax.numpy as jnp
from jax import lax

DATES = 128
COLS = 1024
ROWS = 256


def draw_slc(key, part):
    key = jax.random.fold_in(key, 11)
    keys = jax.random.split(key, 7)
    shape = (DATES, ROWS, COLS)
    root_half = math.sqrt(0.5)
    common_re = jax.random.truncated_normal(keys[0], -4.0, 4.0, (ROWS, COLS), jnp.float32) * root_half
    common_im = jax.random.truncated_normal(keys[1], -4.0, 4.0, (ROWS, COLS), jnp.float32) * root_half
    phase = jax.random.uniform(keys[2], (DATES, 1, 1), jnp.float32, -math.pi, math.pi)
    amplitude = jnp.exp(jax.random.uniform(keys[3], (ROWS, COLS), jnp.float32, math.log(0.5), math.log(5.0)))
    weight = jax.random.uniform(keys[4], (DATES, 1, 1), jnp.float32, 0.2, 0.9)
    noise_re = jax.random.truncated_normal(keys[5], -4.0, 4.0, shape, jnp.float32) * root_half
    noise_im = jax.random.truncated_normal(keys[6], -4.0, 4.0, shape, jnp.float32) * root_half
    cosine = jnp.cos(phase)
    sine = jnp.sin(phase)
    spread = jnp.sqrt(1.0 - weight * weight)
    real_part = amplitude * (weight * (common_re * cosine - common_im * sine) + spread * noise_re)
    imag_part = amplitude * (weight * (common_re * sine + common_im * cosine) + spread * noise_im)
    return jnp.stack([real_part, imag_part]).astype(jnp.bfloat16)


def setup_inputs(seed: int = 0) -> dict:
    seeds = jax.random.split(jax.random.key(seed), 2)
    slc = draw_slc(jax.random.fold_in(seeds[1], 71), 0)
    return dict(slc=slc)


def box_sum(values):
    out_rows = values.shape[-2] // 8
    out_cols = values.shape[-1] // 8
    widths = [(0, 0)] * (values.ndim - 2) + [(3, 4), (3, 4)]
    padded = jnp.pad(values, widths)
    across = sum((padded[..., offset:offset + 8 * (out_cols - 1) + 1:8] for offset in range(15)))
    return sum((across[..., offset:offset + 8 * (out_rows - 1) + 1:8, :] for offset in range(15)))

def reference(slc):
    other_re = slc[0].astype(jnp.float32)
    other_im = slc[1].astype(jnp.float32)

    def one_date(date_index):
        own_re = other_re[date_index][None]
        own_im = other_im[date_index][None]
        real_part = (own_re * other_re + own_im * other_im).astype(jnp.bfloat16)
        imag_part = (own_im * other_re - own_re * other_im).astype(jnp.bfloat16)
        real_part = lax.optimization_barrier(real_part).astype(jnp.float32)
        imag_part = lax.optimization_barrier(imag_part).astype(jnp.float32)
        return jnp.stack([box_sum(real_part), box_sum(imag_part)])
    sums = lax.map(one_date, jnp.arange(DATES))
    sums = jnp.moveaxis(sums, 0, 1)
    power = jnp.moveaxis(jnp.diagonal(sums[0], axis1=0, axis2=1), -1, 0)
    scale = lax.rsqrt(power + 1e-06)
    return sums * scale[None, :, None] * scale[None, None, :]
```

```python
import jax
import jax.numpy as jnp
import numpy as np
from jax import lax
from jax.experimental import pallas as pl
from jax.experimental.pallas import tpu as pltpu
from jax.sharding import PartitionSpec as P

BF16 = jnp.bfloat16
F32 = jnp.float32
LANES = 128
TILES = 5


def iota(shape, axis):
    return lax.broadcasted_iota(jnp.int32, shape, axis)


def butterfly(vregs, group, lane):
    count = len(vregs)
    step = 1
    while step < count:
        upper = (lane // group) & step != 0
        shift = group * step
        for i in range(count):
            if i & step:
                continue
            a, b = vregs[i], vregs[i + step]
            vregs[i] = jnp.where(upper, pltpu.roll(b, shift, 1), a)
            vregs[i + step] = jnp.where(upper, b, pltpu.roll(a, LANES - shift, 1))
        step *= 2
    return vregs


def pack_kernel(own_ref, out_ref):
    dates = own_ref.shape[0] // 16
    chunks = own_ref.shape[1] // LANES
    parts = out_ref.shape[0] // dates
    even = lax.axis_index("row") % 2 == 0
    lane = iota((dates, LANES), 1)
    target, source = iota((16 * dates, 16 * dates), 0), iota((16 * dates, 16 * dates), 1)
    order = (source == target % dates * 16 + target // dates).astype(F32).astype(BF16)
    bands = [[] for _ in range(4)]
    for c in range(0, chunks, 2):
        block = own_ref[:, LANES * c:LANES * (c + 2)]
        moved = jnp.dot(order, block, preferred_element_type=F32)
        for half in range(2):
            chunk = moved[:, LANES * half:LANES * (half + 1)]
            for g in range(4):
                rows = [chunk[dates * r:dates * (r + 1)] for r in range(4 * g, 4 * g + 4)]
                bands[g] += butterfly(rows, 32, lane)
    zero = jnp.zeros((dates, LANES), F32)
    low = lane % 8 < 4
    slot = jnp.where(low, lane // 8 % 4, (lane // 8 + 1) % 4)
    for j in range(parts):
        edge = None
        for g in range(4):
            after = zero if j == parts - 1 else bands[g][j + 1]
            before = zero if j == 0 else bands[g][j - 1]
            both = jnp.where(low, after, before)
            both = pltpu.roll(both, 8 * g, 1) if g else both
            edge = both if edge is None else jnp.where(slot == g, both, edge)
        first, last = bands[0][j], bands[3][j]
        inner, outer = jnp.where(even, last, first), jnp.where(even, first, last)
        tiles = [inner, edge, outer, bands[1][j], bands[2][j]]
        out_ref[pl.ds(dates * j, dates), :] = jnp.concatenate(tiles, axis=1).astype(BF16)


NEAR, FAR = 0, 1
OWN_TILES = ((0, 1, 3, 4), (1, 2, 3, 4))


def window_masks():
    lane = np.arange(LANES)
    sub, c = lane // 8 % 4, lane % 8
    band = np.where(c < 4, sub, (sub + 1) % 4)
    inner = np.where((c < 4) | (band == 0), lane // 32, (lane // 32 - 1) % 4)
    edge = (4 * band + inner, np.where(c < 4, 32 + c, c - 8))
    plain = [(4 * g + lane // 32, lane % 32) for g in range(4)]
    masks = np.zeros((2, 2, 4, 6, LANES), np.float32)
    for odd in range(2):
        own = [plain[0 if odd else 3], edge, plain[3 if odd else 0], plain[1], plain[2]]
        other = [plain[3 if odd else 0], edge, plain[0 if odd else 3]]
        for phase in (NEAR, FAR):
            y = 1 - odd if phase == NEAR else odd
            shift = 16 if y else -16
            halo = other[:2] if phase == NEAR else other[1:]
            tiles = [own[t] for t in OWN_TILES[phase]] + [(r + shift, k) for r, k in halo]
            for x in range(4):
                for t, (row, col) in enumerate(tiles):
                    inside = (row >= 8 * y - 3) & (row <= 8 * y + 11) & (col >= 8 * x - 3) & (col <= 8 * x + 11)
                    masks[odd, phase, x, t] = inside
    assert (masks.sum(axis=(3, 4)) == 225).all()
    return masks.reshape(2, 8, 6 * LANES)


def encode(value):
    value = value * 32768.0
    square = value * value
    fourth = square * square
    return fourth * square * (value * jnp.abs(value))


def decode(code):
    size = jnp.abs(code)
    root = lax.rsqrt(lax.rsqrt(jnp.maximum(size, 1.2e-38)))
    root = root * lax.rsqrt(root) * (1.0 / 32768.0)
    root = jnp.where(size == 0.0, 0.0, root)
    return jnp.where(code < 0.0, -root, root)


def matrices(rows):
    target, source = iota((rows // 2, rows), 0), iota((rows // 2, rows), 1)
    place = target // 4 * 8 + target % 4
    pick_re = (source == place).astype(F32)
    pick_im = (source == place + 4).astype(F32)
    target, source = iota((rows, rows), 0), iota((rows, rows), 1)
    first = target % 8 < 4
    turn = jnp.where(first & (source == target + 4), 1.0, 0.0) - jnp.where(~first & (source == target - 4), 1.0, 0.0)
    return jnp.concatenate([turn, pick_re, pick_im], axis=0).astype(BF16)


def views(samples):
    return jnp.dot(matrices(samples.shape[0]), samples, preferred_element_type=F32).astype(BF16)


def products(samples, view, masks):
    rows = samples.shape[0]
    dates = rows // 2
    left = jnp.concatenate([samples, view[:rows]], axis=1)
    right = jnp.concatenate([view[rows:rows + dates], view[rows + dates:]], axis=1)
    both = jnp.concatenate([right * jnp.concatenate([mask, mask], axis=1) for mask in masks], axis=0)
    return lax.dot_general(left, both, (((1,), (1,)), ((), ())), preferred_element_type=F32)


def chosen(array, which):
    return jnp.concatenate([array[:, LANES * t:LANES * (t + 1)] for t in which], axis=1)


def mask_pair(masks_ref, phase, half):
    odd = lax.axis_index("row") % 2
    return [masks_ref[odd, pl.ds(4 * phase + 2 * half + x, 1), :].astype(BF16) for x in range(2)]


def coded(sums, own, own_re):
    rows, dates = own.shape
    codes = []
    for x in range(2):
        part = sums[:, dates * x:dates * (x + 1)]
        power = jnp.sum(jnp.where(own_re, part, 0.0), axis=0, keepdims=True)
        scale = lax.rsqrt(power + 1e-06)
        own_scale = jnp.sum(jnp.where(own, scale, 0.0), axis=1, keepdims=True)
        codes.append(encode(part * own_scale * scale).reshape(rows // 8, 8, dates))
    return jnp.concatenate(codes, axis=1).astype(BF16)


def own_kernel(samples_ref, masks_ref, sums_ref, near_ref):
    near_ref[...] = samples_ref[:, :2 * LANES]
    width = len(OWN_TILES[NEAR]) * LANES
    samples = samples_ref[...]
    view = views(samples)
    for phase in (NEAR, FAR):
        for half in range(2):
            masks = [mask[:, :width] for mask in mask_pair(masks_ref, phase, half)]
            tiles = OWN_TILES[phase]
            sums_ref[2 * phase + half] = products(chosen(samples, tiles), chosen(view, tiles), masks)


def finish_kernel(sums_ref, near_ref, far_ref, masks_ref, out_ref):
    width = len(OWN_TILES[FAR]) * LANES
    rows = near_ref.shape[0]
    dates = rows // 2
    target, source = iota((rows, dates), 0), iota((rows, dates), 1)
    own = target // 8 * 4 + target % 4 == source
    own_re = own & (target % 8 < 4)
    halos = jnp.concatenate([near_ref[...], far_ref[...]], axis=1)
    halo_views = views(halos)
    for phase in (NEAR, FAR):
        part = slice(2 * LANES * phase, 2 * LANES * (phase + 1))
        for half in range(2):
            masks = [mask[:, width:] for mask in mask_pair(masks_ref, phase, half)]
            group = 2 * phase + half
            sums = sums_ref[group] + products(halos[:, part], halo_views[:, part], masks)
            out_ref[:, 16 * group:16 * (group + 1), :] = coded(sums, own, own_re)


def spread_kernel(codes_ref, out_ref, codes, results, sems):
    parts = codes_ref.shape[0] // 64
    dates = codes_ref.shape[1]
    odd = lax.axis_index("row") % 2
    codes[...] = codes_ref[...].astype(F32)
    source, target = iota((8 * parts, 8 * parts), 0), iota((8 * parts, 8 * parts), 1)
    cols = 4 * parts
    phase = (target // cols + odd + 1) % 2
    wanted = target % cols // 4 * 8 + phase * 4 + target % 4
    order = (source == wanted).astype(F32).astype(BF16)
    copies = []
    for k in range(8):
        block = codes[pl.ds(k, 8 * parts, stride=8), :].astype(BF16)
        moved = lax.dot_general(block, order, (((0,), (0,)), ((), ())), preferred_element_type=F32)
        moved = decode(moved)
        for y in range(2):
            results[k, pl.ds(y, dates, stride=2), :] = moved[:, cols * y:cols * (y + 1)]
        copies.append(pltpu.make_async_copy(results.at[k], out_ref.at[k], sems.at[k]))
        copies[k].start()
    for copy in copies:
        copy.wait()


VMEM = pl.BlockSpec(memory_space=pltpu.VMEM)
HBM = pl.BlockSpec(memory_space=pltpu.HBM)


def call(kernel, name, shapes, scratch=(), flops=0, outputs=VMEM):
    def run(*arrays):
        return pl.pallas_call(
            kernel,
            out_shape=[jax.ShapeDtypeStruct(*shape) for shape in shapes],
            in_specs=[VMEM] * len(arrays),
            out_specs=[outputs] * len(shapes),
            scratch_shapes=list(scratch),
            compiler_params=pltpu.CompilerParams(vmem_limit_bytes=32 * 1024 * 1024),
            cost_estimate=pl.CostEstimate(flops=flops, bytes_accessed=1 << 20, transcendentals=0),
            name=name,
        )(*arrays)

    return run


def on_device(slc):
    dates = slc.shape[1]
    rows, cols = slc.shape[2], slc.shape[3]
    groups = lax.axis_size("row")
    parts = lax.axis_size("date")
    total = parts * dates
    width = TILES * LANES
    own = slc.reshape(2 * dates * rows, cols)
    lines = parts * 2 * dates
    chunks = cols // LANES
    (packed,) = call(pack_kernel, "pack", [((lines, width), BF16)])(own)

    def exchange(array):
        blocks = array.reshape(parts, array.size // parts // array.shape[-1], array.shape[-1])
        return lax.all_to_all(blocks, "date", 0, 0, tiled=True).reshape(-1, array.shape[-1])

    def swapped(array, first):
        pairs = [(i, i + 1) for i in range(first, groups - 1, 2)]
        return lax.ppermute(array, "row", pairs + [(j, i) for i, j in pairs])

    samples = exchange(packed)
    far = swapped(samples[:, LANES:3 * LANES], 1)
    masks = jnp.asarray(window_masks())
    sums, message = call(
        own_kernel, "own", [((4, lines, 2 * total), F32), ((lines, 2 * LANES), BF16)], flops=1 << 30
    )(samples, masks)
    near = swapped(message, 0)
    (codes,) = call(finish_kernel, "finish", [((parts, 64, total), BF16)], flops=1 << 30)(sums, near, far, masks)
    codes = exchange(codes)
    (out,) = call(
        spread_kernel, "spread", [((2 * dates, 2 * total, chunks * 16), F32)],
        [
            pltpu.VMEM((parts * 64, total), F32),
            pltpu.VMEM((2 * dates, 2 * total, chunks * 16), F32),
            pltpu.SemaphoreType.DMA((2 * dates,)),
        ],
        outputs=HBM,
    )(codes)
    return out.reshape(2, dates, total, rows // 8, cols // 8)


def solution(mesh):
    return jax.shard_map(
        on_device,
        mesh=mesh,
        in_specs=(P(None, "date", "row", None),),
        out_specs=P(None, "date", None, "row", None),
        check_vma=False,
    )
```

```python
import jax
import jax.numpy as jnp
import numpy as np
from jax import lax
from jax.experimental import pallas as pl
from jax.experimental.pallas import tpu as pltpu
from jax.sharding import PartitionSpec as P

BF16 = jnp.bfloat16
F32 = jnp.float32
LANES = 128
TILES = 5


def iota(shape, axis):
    return lax.broadcasted_iota(jnp.int32, shape, axis)


def butterfly(vregs, group, lane):
    count = len(vregs)
    step = 1
    while step < count:
        upper = (lane // group) & step != 0
        shift = group * step
        for i in range(count):
            if i & step:
                continue
            a, b = vregs[i], vregs[i + step]
            vregs[i] = jnp.where(upper, pltpu.roll(b, shift, 1), a)
            vregs[i + step] = jnp.where(upper, b, pltpu.roll(a, LANES - shift, 1))
        step *= 2
    return vregs


def folded(parts):
    lane = iota(parts[0].shape, 1)
    slot = jnp.where(lane % 8 < 4, lane // 8 % 4, (lane // 8 + 1) % 4)
    whole = parts[0]
    for q in range(1, 4):
        whole = jnp.where(slot == q, pltpu.roll(parts[q], 8 * q, 1), whole)
    return whole


def pack_kernel(own_ref, out_ref):
    dates = own_ref.shape[0] // 16
    chunks = own_ref.shape[1] // LANES
    parts = out_ref.shape[0] // dates
    even = lax.axis_index("row") % 2 == 0
    lane = iota((dates, LANES), 1)
    target, source = iota((16 * dates, 16 * dates), 0), iota((16 * dates, 16 * dates), 1)
    order = (source == target % dates * 16 + target // dates).astype(F32).astype(BF16)
    bands = [[] for _ in range(4)]
    for c in range(0, chunks, 2):
        block = own_ref[:, LANES * c:LANES * (c + 2)]
        moved = jnp.dot(order, block, preferred_element_type=F32)
        for half in range(2):
            chunk = moved[:, LANES * half:LANES * (half + 1)]
            for g in range(4):
                rows = [chunk[dates * r:dates * (r + 1)] for r in range(4 * g, 4 * g + 4)]
                bands[g] += butterfly(rows, 32, lane)
    zero = jnp.zeros((dates, LANES), F32)
    low = lane % 8 < 4
    for j in range(parts):
        edges = []
        for g in range(4):
            after = zero if j == parts - 1 else bands[g][j + 1]
            before = zero if j == 0 else bands[g][j - 1]
            edges.append(jnp.where(low, after, before))

        def sides(first, last):
            return jnp.where(even, first, last), jnp.where(even, last, first)

        outer, inner = sides(bands[0][j], bands[3][j])
        edge = folded([*sides(edges[0], edges[3]), edges[1], edges[2]])
        tiles = [inner, edge, outer, bands[1][j], bands[2][j]]
        out_ref[pl.ds(dates * j, dates), :] = jnp.concatenate(tiles, axis=1).astype(BF16)


NEAR, FAR = 0, 1
OWN_TILES = ((0, 1, 3, 4), (1, 2, 3, 4))


def window_masks():
    lane = np.arange(LANES)
    sub, c = lane // 8 % 4, lane % 8
    role = np.where(c < 4, sub, (sub + 1) % 4)
    inner = np.where((c < 4) | (role == 0), lane // 32, (lane // 32 - 1) % 4)
    edges = []
    for odd in range(2):
        band = np.array([3, 0, 1, 2] if odd else [0, 3, 1, 2])[role]
        edges.append((4 * band + inner, np.where(c < 4, 32 + c, c - 8)))
    plain = [(4 * g + lane // 32, lane % 32) for g in range(4)]
    masks = np.zeros((2, 2, 4, 6, LANES), np.float32)
    for odd in range(2):
        own = [plain[0 if odd else 3], edges[odd], plain[3 if odd else 0], plain[1], plain[2]]
        other = [plain[3 if odd else 0], edges[1 - odd], plain[0 if odd else 3]]
        for phase in (NEAR, FAR):
            y = 1 - odd if phase == NEAR else odd
            shift = 16 if y else -16
            halo = other[:2] if phase == NEAR else other[1:]
            tiles = [own[t] for t in OWN_TILES[phase]] + [(r + shift, k) for r, k in halo]
            for x in range(4):
                for t, (row, col) in enumerate(tiles):
                    inside = (row >= 8 * y - 3) & (row <= 8 * y + 11) & (col >= 8 * x - 3) & (col <= 8 * x + 11)
                    masks[odd, phase, x, t] = inside
    assert (masks.sum(axis=(3, 4)) == 225).all()
    return masks.reshape(2, 8, 6 * LANES)


def encode(value):
    value = value * 32768.0
    square = value * value
    fourth = square * square
    return fourth * square * (value * jnp.abs(value))


def decode(code):
    size = jnp.abs(code)
    root = lax.rsqrt(lax.rsqrt(jnp.maximum(size, 1.2e-38)))
    root = root * lax.rsqrt(root) * (1.0 / 32768.0)
    root = jnp.where(size == 0.0, 0.0, root)
    return jnp.where(code < 0.0, -root, root)


def matrices(rows):
    target, source = iota((rows // 2, rows), 0), iota((rows // 2, rows), 1)
    place = target // 4 * 8 + target % 4
    pick_re = (source == place).astype(F32)
    pick_im = (source == place + 4).astype(F32)
    target, source = iota((rows, rows), 0), iota((rows, rows), 1)
    first = target % 8 < 4
    turn = jnp.where(first & (source == target + 4), 1.0, 0.0) - jnp.where(~first & (source == target - 4), 1.0, 0.0)
    return jnp.concatenate([turn, pick_re, pick_im], axis=0).astype(BF16)


def views(samples):
    return jnp.dot(matrices(samples.shape[0]), samples, preferred_element_type=F32).astype(BF16)


def products(samples, view, masks):
    rows = samples.shape[0]
    dates = rows // 2
    left = jnp.concatenate([samples, view[:rows]], axis=1)
    right = jnp.concatenate([view[rows:rows + dates], view[rows + dates:]], axis=1)
    both = jnp.concatenate([right * jnp.concatenate([mask, mask], axis=1) for mask in masks], axis=0)
    return lax.dot_general(left, both, (((1,), (1,)), ((), ())), preferred_element_type=F32)


def chosen(array, which):
    return jnp.concatenate([array[:, LANES * t:LANES * (t + 1)] for t in which], axis=1)


def mask_pair(masks_ref, phase, half):
    odd = lax.axis_index("row") % 2
    return [masks_ref[odd, pl.ds(4 * phase + 2 * half + x, 1), :].astype(BF16) for x in range(2)]


def coded(sums, own, own_re):
    rows, dates = own.shape
    codes = []
    for x in range(2):
        part = sums[:, dates * x:dates * (x + 1)]
        power = jnp.sum(jnp.where(own_re, part, 0.0), axis=0, keepdims=True)
        scale = lax.rsqrt(power + 1e-06)
        own_scale = jnp.sum(jnp.where(own, scale, 0.0), axis=1, keepdims=True)
        codes.append(encode(part * own_scale * scale).reshape(rows // 8, 8, dates))
    return jnp.concatenate(codes, axis=1).astype(BF16)


def message_kernel(samples_ref, far_ref, near_ref):
    rows = samples_ref.shape[0]
    edge = samples_ref[:, LANES:2 * LANES].astype(F32)
    for out_ref, tile, lanes in ((far_ref, 2, 0), (near_ref, 0, 8)):
        out_ref[:rows] = samples_ref[:, LANES * tile:LANES * (tile + 1)]
        parts = [edge[rows // 4 * q:rows // 4 * (q + 1)] for q in range(4)]
        parts = [pltpu.roll(part, LANES - lanes, 1) if lanes else part for part in parts]
        out_ref[rows:] = folded(parts).astype(BF16)


def unfolded(message, lanes):
    rows = message.shape[0] // 5 * 4
    edge = message[rows:].astype(F32)
    turned = [pltpu.roll(edge, (LANES - 8 * q + lanes) % LANES, 1) for q in range(4)]
    return message[:rows], jnp.concatenate(turned, axis=0).astype(BF16)


def own_kernel(samples_ref, masks_ref, sums_ref):
    width = len(OWN_TILES[NEAR]) * LANES
    samples = samples_ref[...]
    view = views(samples)
    for phase in (NEAR, FAR):
        for half in range(2):
            masks = [mask[:, :width] for mask in mask_pair(masks_ref, phase, half)]
            tiles = OWN_TILES[phase]
            sums_ref[2 * phase + half] = products(chosen(samples, tiles), chosen(view, tiles), masks)


def finish_kernel(sums_ref, far_ref, near_ref, masks_ref, out_ref):
    width = len(OWN_TILES[FAR]) * LANES
    rows = near_ref.shape[0] // 5 * 4
    dates = rows // 2
    target, source = iota((rows, dates), 0), iota((rows, dates), 1)
    own = target // 8 * 4 + target % 4 == source
    own_re = own & (target % 8 < 4)
    inner, inner_edge = unfolded(near_ref[...], 8)
    outer, outer_edge = unfolded(far_ref[...], 0)
    halos = jnp.concatenate([inner, inner_edge, outer_edge, outer], axis=1)
    halo_views = views(halos)
    for phase in (NEAR, FAR):
        part = slice(2 * LANES * phase, 2 * LANES * (phase + 1))
        for half in range(2):
            masks = [mask[:, width:] for mask in mask_pair(masks_ref, phase, half)]
            group = 2 * phase + half
            sums = sums_ref[group] + products(halos[:, part], halo_views[:, part], masks)
            out_ref[:, 16 * group:16 * (group + 1), :] = coded(sums, own, own_re)


def spread_kernel(codes_ref, out_ref, codes, results, sems):
    parts = codes_ref.shape[0] // 64
    dates = codes_ref.shape[1]
    odd = lax.axis_index("row") % 2
    codes[...] = codes_ref[...].astype(F32)
    source, target = iota((8 * parts, 8 * parts), 0), iota((8 * parts, 8 * parts), 1)
    cols = 4 * parts
    phase = (target // cols + odd + 1) % 2
    wanted = target % cols // 4 * 8 + phase * 4 + target % 4
    order = (source == wanted).astype(F32).astype(BF16)
    copies = []
    for k in range(8):
        block = codes[pl.ds(k, 8 * parts, stride=8), :].astype(BF16)
        moved = lax.dot_general(block, order, (((0,), (0,)), ((), ())), preferred_element_type=F32)
        moved = decode(moved)
        for y in range(2):
            results[k, pl.ds(y, dates, stride=2), :] = moved[:, cols * y:cols * (y + 1)]
        copies.append(pltpu.make_async_copy(results.at[k], out_ref.at[k], sems.at[k]))
        copies[k].start()
    for copy in copies:
        copy.wait()


VMEM = pl.BlockSpec(memory_space=pltpu.VMEM)
HBM = pl.BlockSpec(memory_space=pltpu.HBM)


def call(kernel, name, shapes, scratch=(), flops=0, outputs=VMEM):
    def run(*arrays):
        return pl.pallas_call(
            kernel,
            out_shape=[jax.ShapeDtypeStruct(*shape) for shape in shapes],
            in_specs=[VMEM] * len(arrays),
            out_specs=[outputs] * len(shapes),
            scratch_shapes=list(scratch),
            compiler_params=pltpu.CompilerParams(vmem_limit_bytes=32 * 1024 * 1024),
            cost_estimate=pl.CostEstimate(flops=flops, bytes_accessed=1 << 20, transcendentals=0),
            name=name,
        )(*arrays)

    return run


def on_device(slc):
    dates = slc.shape[1]
    rows, cols = slc.shape[2], slc.shape[3]
    groups = lax.axis_size("row")
    parts = lax.axis_size("date")
    total = parts * dates
    width = TILES * LANES
    own = slc.reshape(2 * dates * rows, cols)
    lines = parts * 2 * dates
    chunks = cols // LANES
    (packed,) = call(pack_kernel, "pack", [((lines, width), BF16)])(own)

    def exchange(array):
        blocks = array.reshape(parts, array.size // parts // array.shape[-1], array.shape[-1])
        return lax.all_to_all(blocks, "date", 0, 0, tiled=True).reshape(-1, array.shape[-1])

    def swapped(array, first):
        pairs = [(i, i + 1) for i in range(first, groups - 1, 2)]
        return lax.ppermute(array, "row", pairs + [(j, i) for i, j in pairs])

    samples = exchange(packed)
    far, near = call(
        message_kernel, "message", [((lines // 4 * 5, LANES), BF16)] * 2
    )(samples)
    far, near = swapped(far, 1), swapped(near, 0)
    masks = jnp.asarray(window_masks())
    (sums,) = call(own_kernel, "own", [((4, lines, 2 * total), F32)], flops=1 << 30)(samples, masks)
    (codes,) = call(finish_kernel, "finish", [((parts, 64, total), BF16)], flops=1 << 30)(sums, far, near, masks)
    codes = exchange(codes)
    (out,) = call(
        spread_kernel, "spread", [((2 * dates, 2 * total, chunks * 16), F32)],
        [
            pltpu.VMEM((parts * 64, total), F32),
            pltpu.VMEM((2 * dates, 2 * total, chunks * 16), F32),
            pltpu.SemaphoreType.DMA((2 * dates,)),
        ],
        outputs=HBM,
    )(codes)
    return out.reshape(2, dates, total, rows // 8, cols // 8)


def solution(mesh):
    return jax.shard_map(
        on_device,
        mesh=mesh,
        in_specs=(P(None, "date", "row", None),),
        out_specs=P(None, "date", None, "row", None),
        check_vma=False,
    )
```

```python
import jax
import jax.numpy as jnp
import numpy as np
from jax import lax
from jax.experimental import pallas as pl
from jax.experimental.pallas import tpu as pltpu
from jax.sharding import PartitionSpec as P

BF16 = jnp.bfloat16
F32 = jnp.float32
LANES = 128
TILES = 5


def iota(shape, axis):
    return lax.broadcasted_iota(jnp.int32, shape, axis)


def butterfly(vregs, group, lane):
    count = len(vregs)
    step = 1
    while step < count:
        upper = (lane // group) & step != 0
        shift = group * step
        for i in range(count):
            if i & step:
                continue
            a, b = vregs[i], vregs[i + step]
            vregs[i] = jnp.where(upper, pltpu.roll(b, shift, 1), a)
            vregs[i + step] = jnp.where(upper, b, pltpu.roll(a, LANES - shift, 1))
        step *= 2
    return vregs


def folded(parts):
    lane = iota(parts[0].shape, 1)
    slot = jnp.where(lane % 8 < 4, lane // 8 % 4, (lane // 8 + 1) % 4)
    whole = parts[0]
    for q in range(1, 4):
        whole = jnp.where(slot == q, pltpu.roll(parts[q], 8 * q, 1), whole)
    return whole


def pack_kernel(own_ref, out_ref):
    dates = own_ref.shape[0] // 16
    chunks = own_ref.shape[1] // LANES
    parts = out_ref.shape[0] // dates
    even = lax.axis_index("row") % 2 == 0
    lane = iota((dates, LANES), 1)
    target, source = iota((16 * dates, 16 * dates), 0), iota((16 * dates, 16 * dates), 1)
    order = (source == target % dates * 16 + target // dates).astype(F32).astype(BF16)
    bands = [[] for _ in range(4)]
    for c in range(0, chunks, 2):
        block = own_ref[:, LANES * c:LANES * (c + 2)]
        moved = jnp.dot(order, block, preferred_element_type=F32)
        for half in range(2):
            chunk = moved[:, LANES * half:LANES * (half + 1)]
            for g in range(4):
                rows = [chunk[dates * r:dates * (r + 1)] for r in range(4 * g, 4 * g + 4)]
                bands[g] += butterfly(rows, 32, lane)
    zero = jnp.zeros((dates, LANES), F32)
    low = lane % 8 < 4
    for j in range(parts):
        edges = []
        for g in range(4):
            after = zero if j == parts - 1 else bands[g][j + 1]
            before = zero if j == 0 else bands[g][j - 1]
            edges.append(jnp.where(low, after, before))

        def sides(first, last):
            return jnp.where(even, first, last), jnp.where(even, last, first)

        outer, inner = sides(bands[0][j], bands[3][j])
        edge = folded([*sides(edges[0], edges[3]), edges[1], edges[2]])
        tiles = [inner, edge, outer, bands[1][j], bands[2][j]]
        out_ref[pl.ds(dates * j, dates), :] = jnp.concatenate(tiles, axis=1).astype(BF16)


NEAR, FAR = 0, 1
OWN_TILES = ((0, 1, 3, 4), (1, 2, 3, 4))


def window_masks():
    lane = np.arange(LANES)
    sub, c = lane // 8 % 4, lane % 8
    role = np.where(c < 4, sub, (sub + 1) % 4)
    inner = np.where((c < 4) | (role == 0), lane // 32, (lane // 32 - 1) % 4)
    edges = []
    for odd in range(2):
        band = np.array([3, 0, 1, 2] if odd else [0, 3, 1, 2])[role]
        edges.append((4 * band + inner, np.where(c < 4, 32 + c, c - 8)))
    plain = [(4 * g + lane // 32, lane % 32) for g in range(4)]
    masks = np.zeros((2, 2, 4, 6, LANES), np.float32)
    for odd in range(2):
        own = [plain[0 if odd else 3], edges[odd], plain[3 if odd else 0], plain[1], plain[2]]
        other = [plain[3 if odd else 0], edges[1 - odd], plain[0 if odd else 3]]
        for phase in (NEAR, FAR):
            y = 1 - odd if phase == NEAR else odd
            shift = 16 if y else -16
            halo = other[:2] if phase == NEAR else other[1:]
            tiles = [own[t] for t in OWN_TILES[phase]] + [(r + shift, k) for r, k in halo]
            for x in range(4):
                for t, (row, col) in enumerate(tiles):
                    inside = (row >= 8 * y - 3) & (row <= 8 * y + 11) & (col >= 8 * x - 3) & (col <= 8 * x + 11)
                    masks[odd, phase, x, t] = inside
    assert (masks.sum(axis=(3, 4)) == 225).all()
    return masks.reshape(2, 8, 6 * LANES)


def encode(value):
    value = value * 131072.0
    square = value * value
    fourth = square * square
    return fourth * square * value


def decode(code):
    size = jnp.abs(code)
    root = lax.exp2(jnp.log(jnp.maximum(size, 1.2e-38)) * (1.0 / (7.0 * np.log(2.0))) - 17.0)
    root = jnp.where(size == 0.0, 0.0, root)
    return jnp.where(code < 0.0, -root, root)


def matrices(rows):
    target, source = iota((rows // 2, rows), 0), iota((rows // 2, rows), 1)
    place = target // 4 * 8 + target % 4
    pick_re = (source == place).astype(F32)
    pick_im = (source == place + 4).astype(F32)
    target, source = iota((rows, rows), 0), iota((rows, rows), 1)
    first = target % 8 < 4
    turn = jnp.where(first & (source == target + 4), 1.0, 0.0) - jnp.where(~first & (source == target - 4), 1.0, 0.0)
    return jnp.concatenate([turn, pick_re, pick_im], axis=0).astype(BF16)


def views(samples):
    return jnp.dot(matrices(samples.shape[0]), samples, preferred_element_type=F32).astype(BF16)


def products(samples, view, masks):
    rows = samples.shape[0]
    dates = rows // 2
    left = jnp.concatenate([samples, view[:rows]], axis=1)
    right = jnp.concatenate([view[rows:rows + dates], view[rows + dates:]], axis=1)
    both = jnp.concatenate([right * jnp.concatenate([mask, mask], axis=1) for mask in masks], axis=0)
    return lax.dot_general(left, both, (((1,), (1,)), ((), ())), preferred_element_type=F32)


def chosen(array, which):
    return jnp.concatenate([array[:, LANES * t:LANES * (t + 1)] for t in which], axis=1)


def mask_pair(masks_ref, phase, half):
    odd = lax.axis_index("row") % 2
    return [masks_ref[odd, pl.ds(4 * phase + 2 * half + x, 1), :].astype(BF16) for x in range(2)]


def coded(sums, own, own_re):
    rows, dates = own.shape
    codes = []
    for x in range(2):
        part = sums[:, dates * x:dates * (x + 1)]
        power = jnp.sum(jnp.where(own_re, part, 0.0), axis=0, keepdims=True)
        scale = lax.rsqrt(power + 1e-06)
        own_scale = jnp.sum(jnp.where(own, scale, 0.0), axis=1, keepdims=True)
        codes.append(encode(part * own_scale * scale).reshape(rows // 8, 8, dates))
    return jnp.concatenate(codes, axis=1).astype(BF16)


def message_kernel(samples_ref, far_ref, near_ref):
    rows = samples_ref.shape[0]
    edge = samples_ref[:, LANES:2 * LANES].astype(F32)
    for out_ref, tile, lanes in ((far_ref, 2, 0), (near_ref, 0, 8)):
        out_ref[:rows] = samples_ref[:, LANES * tile:LANES * (tile + 1)]
        parts = [edge[rows // 4 * q:rows // 4 * (q + 1)] for q in range(4)]
        parts = [pltpu.roll(part, LANES - lanes, 1) if lanes else part for part in parts]
        out_ref[rows:] = folded(parts).astype(BF16)


def unfolded(message, lanes):
    rows = message.shape[0] // 5 * 4
    edge = message[rows:].astype(F32)
    turned = [pltpu.roll(edge, (LANES - 8 * q + lanes) % LANES, 1) for q in range(4)]
    return message[:rows], jnp.concatenate(turned, axis=0).astype(BF16)


def own_kernel(samples_ref, masks_ref, sums_ref):
    width = len(OWN_TILES[NEAR]) * LANES
    samples = samples_ref[...]
    view = views(samples)
    for phase in (NEAR, FAR):
        for half in range(2):
            masks = [mask[:, :width] for mask in mask_pair(masks_ref, phase, half)]
            tiles = OWN_TILES[phase]
            sums_ref[2 * phase + half] = products(chosen(samples, tiles), chosen(view, tiles), masks)


def finish_kernel(sums_ref, far_ref, near_ref, masks_ref, out_ref):
    width = len(OWN_TILES[FAR]) * LANES
    rows = near_ref.shape[0] // 5 * 4
    dates = rows // 2
    target, source = iota((rows, dates), 0), iota((rows, dates), 1)
    own = target // 8 * 4 + target % 4 == source
    own_re = own & (target % 8 < 4)
    inner, inner_edge = unfolded(near_ref[...], 8)
    outer, outer_edge = unfolded(far_ref[...], 0)
    halos = jnp.concatenate([inner, inner_edge, outer_edge, outer], axis=1)
    halo_views = views(halos)
    for phase in (NEAR, FAR):
        part = slice(2 * LANES * phase, 2 * LANES * (phase + 1))
        for half in range(2):
            masks = [mask[:, width:] for mask in mask_pair(masks_ref, phase, half)]
            group = 2 * phase + half
            sums = sums_ref[group] + products(halos[:, part], halo_views[:, part], masks)
            out_ref[:, 16 * group:16 * (group + 1), :] = coded(sums, own, own_re)


def spread_kernel(codes_ref, out_ref, codes, results, sems):
    parts = codes_ref.shape[0] // 64
    dates = codes_ref.shape[1]
    odd = lax.axis_index("row") % 2
    codes[...] = codes_ref[...].astype(F32)
    source, target = iota((8 * parts, 8 * parts), 0), iota((8 * parts, 8 * parts), 1)
    cols = 4 * parts
    phase = (target // cols + odd + 1) % 2
    wanted = target % cols // 4 * 8 + phase * 4 + target % 4
    order = (source == wanted).astype(F32).astype(BF16)
    copies = []
    for k in range(8):
        block = codes[pl.ds(k, 8 * parts, stride=8), :].astype(BF16)
        moved = lax.dot_general(block, order, (((0,), (0,)), ((), ())), preferred_element_type=F32)
        moved = decode(moved)
        for y in range(2):
            results[k, pl.ds(y, dates, stride=2), :] = moved[:, cols * y:cols * (y + 1)]
        copies.append(pltpu.make_async_copy(results.at[k], out_ref.at[k], sems.at[k]))
        copies[k].start()
    for copy in copies:
        copy.wait()


VMEM = pl.BlockSpec(memory_space=pltpu.VMEM)
HBM = pl.BlockSpec(memory_space=pltpu.HBM)


def call(kernel, name, shapes, scratch=(), flops=0, outputs=VMEM):
    def run(*arrays):
        return pl.pallas_call(
            kernel,
            out_shape=[jax.ShapeDtypeStruct(*shape) for shape in shapes],
            in_specs=[VMEM] * len(arrays),
            out_specs=[outputs] * len(shapes),
            scratch_shapes=list(scratch),
            compiler_params=pltpu.CompilerParams(vmem_limit_bytes=32 * 1024 * 1024),
            cost_estimate=pl.CostEstimate(flops=flops, bytes_accessed=1 << 20, transcendentals=0),
            name=name,
        )(*arrays)

    return run


def on_device(slc):
    dates = slc.shape[1]
    rows, cols = slc.shape[2], slc.shape[3]
    groups = lax.axis_size("row")
    parts = lax.axis_size("date")
    total = parts * dates
    width = TILES * LANES
    own = slc.reshape(2 * dates * rows, cols)
    lines = parts * 2 * dates
    chunks = cols // LANES
    (packed,) = call(pack_kernel, "pack", [((lines, width), BF16)])(own)

    def exchange(array):
        blocks = array.reshape(parts, array.size // parts // array.shape[-1], array.shape[-1])
        return lax.all_to_all(blocks, "date", 0, 0, tiled=True).reshape(-1, array.shape[-1])

    def swapped(array, first):
        pairs = [(i, i + 1) for i in range(first, groups - 1, 2)]
        return lax.ppermute(array, "row", pairs + [(j, i) for i, j in pairs])

    samples = exchange(packed)
    far, near = call(
        message_kernel, "message", [((lines // 4 * 5, LANES), BF16)] * 2
    )(samples)
    far, near = swapped(far, 1), swapped(near, 0)
    masks = jnp.asarray(window_masks())
    (sums,) = call(own_kernel, "own", [((4, lines, 2 * total), F32)], flops=1 << 30)(samples, masks)
    (codes,) = call(finish_kernel, "finish", [((parts, 64, total), BF16)], flops=1 << 30)(sums, far, near, masks)
    codes = exchange(codes)
    (out,) = call(
        spread_kernel, "spread", [((2 * dates, 2 * total, chunks * 16), F32)],
        [
            pltpu.VMEM((parts * 64, total), F32),
            pltpu.VMEM((2 * dates, 2 * total, chunks * 16), F32),
            pltpu.SemaphoreType.DMA((2 * dates,)),
        ],
        outputs=HBM,
    )(codes)
    return out.reshape(2, dates, total, rows // 8, cols // 8)


def solution(mesh):
    return jax.shard_map(
        on_device,
        mesh=mesh,
        in_specs=(P(None, "date", "row", None),),
        out_specs=P(None, "date", None, "row", None),
        check_vma=False,
    )
```

```python
import jax
import jax.numpy as jnp
import numpy as np
from jax import lax
from jax.experimental import pallas as pl
from jax.experimental.pallas import tpu as pltpu
from jax.sharding import PartitionSpec as P

BF16 = jnp.bfloat16
F32 = jnp.float32
LANES = 128
TILES = 5


def iota(shape, axis):
    return lax.broadcasted_iota(jnp.int32, shape, axis)


def butterfly(vregs, group, lane):
    count = len(vregs)
    step = 1
    while step < count:
        upper = (lane // group) & step != 0
        shift = group * step
        for i in range(count):
            if i & step:
                continue
            a, b = vregs[i], vregs[i + step]
            vregs[i] = jnp.where(upper, pltpu.roll(b, shift, 1), a)
            vregs[i + step] = jnp.where(upper, b, pltpu.roll(a, LANES - shift, 1))
        step *= 2
    return vregs


def folded(parts):
    lane = iota(parts[0].shape, 1)
    slot = jnp.where(lane % 8 < 4, lane // 8 % 4, (lane // 8 + 1) % 4)
    whole = parts[0]
    for q in range(1, 4):
        whole = jnp.where(slot == q, pltpu.roll(parts[q], 8 * q, 1), whole)
    return whole


def pack_kernel(own_ref, out_ref):
    dates = own_ref.shape[0] // 16
    chunks = own_ref.shape[1] // LANES
    parts = out_ref.shape[0] // dates
    even = lax.axis_index("row") % 2 == 0
    lane = iota((dates, LANES), 1)
    target, source = iota((16 * dates, 16 * dates), 0), iota((16 * dates, 16 * dates), 1)
    order = (source == target % dates * 16 + target // dates).astype(F32).astype(BF16)
    bands = [[] for _ in range(4)]
    for c in range(0, chunks, 2):
        block = own_ref[:, LANES * c:LANES * (c + 2)]
        moved = jnp.dot(order, block, preferred_element_type=F32)
        for half in range(2):
            chunk = moved[:, LANES * half:LANES * (half + 1)]
            for g in range(4):
                rows = [chunk[dates * r:dates * (r + 1)] for r in range(4 * g, 4 * g + 4)]
                bands[g] += butterfly(rows, 32, lane)
    zero = jnp.zeros((dates, LANES), F32)
    low = lane % 8 < 4
    for j in range(parts):
        edges = []
        for g in range(4):
            after = zero if j == parts - 1 else bands[g][j + 1]
            before = zero if j == 0 else bands[g][j - 1]
            edges.append(jnp.where(low, after, before))

        def sides(first, last):
            return jnp.where(even, first, last), jnp.where(even, last, first)

        outer, inner = sides(bands[0][j], bands[3][j])
        edge = folded([*sides(edges[0], edges[3]), edges[1], edges[2]])
        tiles = [inner, edge, outer, bands[1][j], bands[2][j]]
        out_ref[pl.ds(dates * j, dates), :] = jnp.concatenate(tiles, axis=1).astype(BF16)


NEAR, FAR = 0, 1
OWN_TILES = ((0, 1, 3, 4), (1, 2, 3, 4))


def window_masks():
    lane = np.arange(LANES)
    sub, c = lane // 8 % 4, lane % 8
    role = np.where(c < 4, sub, (sub + 1) % 4)
    inner = np.where((c < 4) | (role == 0), lane // 32, (lane // 32 - 1) % 4)
    edges = []
    for odd in range(2):
        band = np.array([3, 0, 1, 2] if odd else [0, 3, 1, 2])[role]
        edges.append((4 * band + inner, np.where(c < 4, 32 + c, c - 8)))
    plain = [(4 * g + lane // 32, lane % 32) for g in range(4)]
    masks = np.zeros((2, 2, 4, 6, LANES), np.float32)
    for odd in range(2):
        own = [plain[0 if odd else 3], edges[odd], plain[3 if odd else 0], plain[1], plain[2]]
        other = [plain[3 if odd else 0], edges[1 - odd], plain[0 if odd else 3]]
        for phase in (NEAR, FAR):
            y = 1 - odd if phase == NEAR else odd
            shift = 16 if y else -16
            halo = other[:2] if phase == NEAR else other[1:]
            tiles = [own[t] for t in OWN_TILES[phase]] + [(r + shift, k) for r, k in halo]
            for x in range(4):
                for t, (row, col) in enumerate(tiles):
                    inside = (row >= 8 * y - 3) & (row <= 8 * y + 11) & (col >= 8 * x - 3) & (col <= 8 * x + 11)
                    masks[odd, phase, x, t] = inside
    assert (masks.sum(axis=(3, 4)) == 225).all()
    return masks.reshape(2, 8, 6 * LANES)


def encode(value):
    value = value * 131072.0
    square = value * value
    fourth = square * square
    return fourth * square * value


def decode(code):
    size = jnp.abs(code)
    root = lax.exp2(jnp.log(jnp.maximum(size, 1.2e-38)) * (1.0 / (7.0 * np.log(2.0))) - 17.0)
    root = jnp.where(size == 0.0, 0.0, root)
    return jnp.where(code < 0.0, -root, root)


def matrices(rows):
    target, source = iota((rows // 2, rows), 0), iota((rows // 2, rows), 1)
    place = target // 4 * 8 + target % 4
    pick_re = (source == place).astype(F32)
    pick_im = (source == place + 4).astype(F32)
    target, source = iota((rows, rows), 0), iota((rows, rows), 1)
    first = target % 8 < 4
    turn = jnp.where(first & (source == target + 4), 1.0, 0.0) - jnp.where(~first & (source == target - 4), 1.0, 0.0)
    return jnp.concatenate([turn, pick_re, pick_im], axis=0).astype(BF16)


def views(samples):
    return jnp.dot(matrices(samples.shape[0]), samples, preferred_element_type=F32).astype(BF16)


def products(samples, view, masks):
    rows = samples.shape[0]
    dates = rows // 2
    left = jnp.concatenate([samples, view[:rows]], axis=1)
    right = jnp.concatenate([view[rows:rows + dates], view[rows + dates:]], axis=1)
    both = jnp.concatenate([right * jnp.concatenate([mask, mask], axis=1) for mask in masks], axis=0)
    return lax.dot_general(left, both, (((1,), (1,)), ((), ())), preferred_element_type=F32)


def chosen(array, which):
    return jnp.concatenate([array[:, LANES * t:LANES * (t + 1)] for t in which], axis=1)


def mask_pair(masks_ref, phase, half):
    odd = lax.axis_index("row") % 2
    return [masks_ref[odd, pl.ds(4 * phase + 2 * half + x, 1), :].astype(BF16) for x in range(2)]


def coded(sums, own, own_re):
    rows, dates = own.shape
    codes = []
    for x in range(2):
        part = sums[:, dates * x:dates * (x + 1)]
        power = jnp.sum(jnp.where(own_re, part, 0.0), axis=0, keepdims=True)
        scale = lax.rsqrt(power + 1e-06)
        own_scale = jnp.sum(jnp.where(own, scale, 0.0), axis=1, keepdims=True)
        codes.append(encode(part * own_scale * scale).reshape(rows // 8, 8, dates))
    return jnp.concatenate(codes, axis=1).astype(BF16)


def message_kernel(samples_ref, far_ref, near_ref):
    rows = samples_ref.shape[0]
    edge = samples_ref[:, LANES:2 * LANES].astype(F32)
    for out_ref, tile, lanes in ((far_ref, 2, 0), (near_ref, 0, 8)):
        out_ref[:rows] = samples_ref[:, LANES * tile:LANES * (tile + 1)]
        parts = [edge[rows // 4 * q:rows // 4 * (q + 1)] for q in range(4)]
        parts = [pltpu.roll(part, LANES - lanes, 1) if lanes else part for part in parts]
        out_ref[rows:] = folded(parts).astype(BF16)


def unfolded(message, lanes):
    rows = message.shape[0] // 5 * 4
    edge = message[rows:].astype(F32)
    turned = [pltpu.roll(edge, (LANES - 8 * q + lanes) % LANES, 1) for q in range(4)]
    return message[:rows], jnp.concatenate(turned, axis=0).astype(BF16)


def own_kernel(samples_ref, masks_ref, sums_ref):
    width = len(OWN_TILES[NEAR]) * LANES
    samples = samples_ref[...]
    view = views(samples)
    for phase in (NEAR, FAR):
        for half in range(2):
            masks = [mask[:, :width] for mask in mask_pair(masks_ref, phase, half)]
            tiles = OWN_TILES[phase]
            sums_ref[2 * phase + half] = products(chosen(samples, tiles), chosen(view, tiles), masks)


def finish_kernel(sums_ref, far_ref, near_ref, masks_ref, out_ref):
    width = len(OWN_TILES[FAR]) * LANES
    rows = near_ref.shape[0] // 5 * 4
    dates = rows // 2
    target, source = iota((rows, dates), 0), iota((rows, dates), 1)
    own = target // 8 * 4 + target % 4 == source
    own_re = own & (target % 8 < 4)
    inner, inner_edge = unfolded(near_ref[...], 8)
    outer, outer_edge = unfolded(far_ref[...], 0)
    halos = jnp.concatenate([inner, inner_edge, outer_edge, outer], axis=1)
    halo_views = views(halos)
    for phase in (NEAR, FAR):
        part = slice(2 * LANES * phase, 2 * LANES * (phase + 1))
        for half in range(2):
            masks = [mask[:, width:] for mask in mask_pair(masks_ref, phase, half)]
            group = 2 * phase + half
            sums = sums_ref[group] + products(halos[:, part], halo_views[:, part], masks)
            out_ref[:, 16 * group:16 * (group + 1), :] = coded(sums, own, own_re)


def spread_kernel(codes_ref, out_ref, codes, results, sems):
    parts = codes_ref.shape[0] // 64
    dates = codes_ref.shape[1]
    odd = lax.axis_index("row") % 2
    codes[...] = codes_ref[...].astype(F32)
    source, target = iota((8 * parts, 8 * parts), 0), iota((8 * parts, 8 * parts), 1)
    cols = 4 * parts
    phase = (target // cols + odd + 1) % 2
    wanted = target % cols // 4 * 8 + phase * 4 + target % 4
    order = (source == wanted).astype(F32).astype(BF16)
    copies = []
    for k in range(8):
        block = codes[pl.ds(k, 8 * parts, stride=8), :].astype(BF16)
        moved = lax.dot_general(block, order, (((0,), (0,)), ((), ())), preferred_element_type=F32)
        moved = decode(moved)
        for y in range(2):
            results[k, pl.ds(y, dates, stride=2), :] = moved[:, cols * y:cols * (y + 1)]
        if k % 2:
            pair = pl.ds(k - 1, 2)
            copies.append(pltpu.make_async_copy(results.at[pair], out_ref.at[pair], sems.at[k // 2]))
            copies[-1].start()
    for copy in copies:
        copy.wait()


VMEM = pl.BlockSpec(memory_space=pltpu.VMEM)
HBM = pl.BlockSpec(memory_space=pltpu.HBM)


def call(kernel, name, shapes, scratch=(), flops=0, outputs=VMEM):
    def run(*arrays):
        return pl.pallas_call(
            kernel,
            out_shape=[jax.ShapeDtypeStruct(*shape) for shape in shapes],
            in_specs=[VMEM] * len(arrays),
            out_specs=[outputs] * len(shapes),
            scratch_shapes=list(scratch),
            compiler_params=pltpu.CompilerParams(vmem_limit_bytes=32 * 1024 * 1024),
            cost_estimate=pl.CostEstimate(flops=flops, bytes_accessed=1 << 20, transcendentals=0),
            name=name,
        )(*arrays)

    return run


def on_device(slc):
    dates = slc.shape[1]
    rows, cols = slc.shape[2], slc.shape[3]
    groups = lax.axis_size("row")
    parts = lax.axis_size("date")
    total = parts * dates
    width = TILES * LANES
    own = slc.reshape(2 * dates * rows, cols)
    lines = parts * 2 * dates
    chunks = cols // LANES
    (packed,) = call(pack_kernel, "pack", [((lines, width), BF16)])(own)

    def exchange(array):
        blocks = array.reshape(parts, array.size // parts // array.shape[-1], array.shape[-1])
        return lax.all_to_all(blocks, "date", 0, 0, tiled=True).reshape(-1, array.shape[-1])

    def swapped(array, first):
        pairs = [(i, i + 1) for i in range(first, groups - 1, 2)]
        return lax.ppermute(array, "row", pairs + [(j, i) for i, j in pairs])

    samples = exchange(packed)
    far, near = call(
        message_kernel, "message", [((lines // 4 * 5, LANES), BF16)] * 2
    )(samples)
    far, near = swapped(far, 1), swapped(near, 0)
    masks = jnp.asarray(window_masks())
    (sums,) = call(own_kernel, "own", [((4, lines, 2 * total), F32)], flops=1 << 30)(samples, masks)
    (codes,) = call(finish_kernel, "finish", [((parts, 64, total), BF16)], flops=1 << 30)(sums, far, near, masks)
    codes = exchange(codes)
    (out,) = call(
        spread_kernel, "spread", [((2 * dates, 2 * total, chunks * 16), F32)],
        [
            pltpu.VMEM((parts * 64, total), F32),
            pltpu.VMEM((2 * dates, 2 * total, chunks * 16), F32),
            pltpu.SemaphoreType.DMA((dates,)),
        ],
        outputs=HBM,
    )(codes)
    return out.reshape(2, dates, total, rows // 8, cols // 8)


def solution(mesh):
    return jax.shard_map(
        on_device,
        mesh=mesh,
        in_specs=(P(None, "date", "row", None),),
        out_specs=P(None, "date", None, "row", None),
        check_vma=False,
    )
```

```python
import jax
import jax.numpy as jnp
import numpy as np
from jax import lax
from jax.experimental import pallas as pl
from jax.experimental.pallas import tpu as pltpu
from jax.sharding import PartitionSpec as P

BF16 = jnp.bfloat16
F32 = jnp.float32
LANES = 128
TILES = 5


def iota(shape, axis):
    return lax.broadcasted_iota(jnp.int32, shape, axis)


def butterfly(vregs, group, lane):
    count = len(vregs)
    step = 1
    while step < count:
        upper = (lane // group) & step != 0
        shift = group * step
        for i in range(count):
            if i & step:
                continue
            a, b = vregs[i], vregs[i + step]
            vregs[i] = jnp.where(upper, pltpu.roll(b, shift, 1), a)
            vregs[i + step] = jnp.where(upper, b, pltpu.roll(a, LANES - shift, 1))
        step *= 2
    return vregs


def folded(parts):
    lane = iota(parts[0].shape, 1)
    slot = jnp.where(lane % 8 < 4, lane // 8 % 4, (lane // 8 + 1) % 4)
    whole = parts[0]
    for q in range(1, 4):
        whole = jnp.where(slot == q, pltpu.roll(parts[q], 8 * q, 1), whole)
    return whole


def pack_kernel(own_ref, out_ref):
    dates = own_ref.shape[0] // 16
    chunks = own_ref.shape[1] // LANES
    parts = out_ref.shape[0] // dates
    even = lax.axis_index("row") % 2 == 0
    lane = iota((dates, LANES), 1)
    target, source = iota((16 * dates, 16 * dates), 0), iota((16 * dates, 16 * dates), 1)
    order = (source == target % dates * 16 + target // dates).astype(F32).astype(BF16)
    bands = [[] for _ in range(4)]
    for c in range(0, chunks, 2):
        block = own_ref[:, LANES * c:LANES * (c + 2)]
        moved = jnp.dot(order, block, preferred_element_type=F32)
        for half in range(2):
            chunk = moved[:, LANES * half:LANES * (half + 1)]
            for g in range(4):
                rows = [chunk[dates * r:dates * (r + 1)] for r in range(4 * g, 4 * g + 4)]
                bands[g] += butterfly(rows, 32, lane)
    zero = jnp.zeros((dates, LANES), F32)
    low = lane % 8 < 4
    for j in range(parts):
        edges = []
        for g in range(4):
            after = zero if j == parts - 1 else bands[g][j + 1]
            before = zero if j == 0 else bands[g][j - 1]
            edges.append(jnp.where(low, after, before))

        def sides(first, last):
            return jnp.where(even, first, last), jnp.where(even, last, first)

        outer, inner = sides(bands[0][j], bands[3][j])
        edge = folded([*sides(edges[0], edges[3]), edges[1], edges[2]])
        tiles = [inner, edge, outer, bands[1][j], bands[2][j]]
        out_ref[pl.ds(dates * j, dates), :] = jnp.concatenate(tiles, axis=1).astype(BF16)


NEAR, FAR = 0, 1
OWN_TILES = ((0, 1, 3, 4), (1, 2, 3, 4))


def window_masks():
    lane = np.arange(LANES)
    sub, c = lane // 8 % 4, lane % 8
    role = np.where(c < 4, sub, (sub + 1) % 4)
    inner = np.where((c < 4) | (role == 0), lane // 32, (lane // 32 - 1) % 4)
    edges = []
    for odd in range(2):
        band = np.array([3, 0, 1, 2] if odd else [0, 3, 1, 2])[role]
        edges.append((4 * band + inner, np.where(c < 4, 32 + c, c - 8)))
    plain = [(4 * g + lane // 32, lane % 32) for g in range(4)]
    masks = np.zeros((2, 2, 4, 6, LANES), np.float32)
    for odd in range(2):
        own = [plain[0 if odd else 3], edges[odd], plain[3 if odd else 0], plain[1], plain[2]]
        other = [plain[3 if odd else 0], edges[1 - odd], plain[0 if odd else 3]]
        for phase in (NEAR, FAR):
            y = 1 - odd if phase == NEAR else odd
            shift = 16 if y else -16
            halo = other[:2] if phase == NEAR else other[1:]
            tiles = [own[t] for t in OWN_TILES[phase]] + [(r + shift, k) for r, k in halo]
            for x in range(4):
                for t, (row, col) in enumerate(tiles):
                    inside = (row >= 8 * y - 3) & (row <= 8 * y + 11) & (col >= 8 * x - 3) & (col <= 8 * x + 11)
                    masks[odd, phase, x, t] = inside
    assert (masks.sum(axis=(3, 4)) == 225).all()
    return masks.reshape(2, 8, 6 * LANES)


def encode(value):
    value = value * 131072.0
    square = value * value
    fourth = square * square
    return fourth * square * value


def decode(code):
    size = jnp.abs(code)
    root = lax.exp2(jnp.log(jnp.maximum(size, 1.2e-38)) * (1.0 / (7.0 * np.log(2.0))) - 17.0)
    root = jnp.where(size == 0.0, 0.0, root)
    return jnp.where(code < 0.0, -root, root)


def matrices(rows):
    target, source = iota((rows // 2, rows), 0), iota((rows // 2, rows), 1)
    place = target // 4 * 8 + target % 4
    pick_re = (source == place).astype(F32)
    pick_im = (source == place + 4).astype(F32)
    target, source = iota((rows, rows), 0), iota((rows, rows), 1)
    first = target % 8 < 4
    turn = jnp.where(first & (source == target + 4), 1.0, 0.0) - jnp.where(~first & (source == target - 4), 1.0, 0.0)
    return jnp.concatenate([turn, pick_re, pick_im], axis=0).astype(BF16)


def views(samples):
    return jnp.dot(matrices(samples.shape[0]), samples, preferred_element_type=F32).astype(BF16)


def products(samples, view, masks):
    rows = samples.shape[0]
    dates = rows // 2
    left = jnp.concatenate([samples, view[:rows]], axis=1)
    right = jnp.concatenate([view[rows:rows + dates], view[rows + dates:]], axis=1)
    both = jnp.concatenate([right * jnp.concatenate([mask, mask], axis=1) for mask in masks], axis=0)
    return lax.dot_general(left, both, (((1,), (1,)), ((), ())), preferred_element_type=F32)


def chosen(array, which):
    return jnp.concatenate([array[:, LANES * t:LANES * (t + 1)] for t in which], axis=1)


def mask_pair(masks_ref, phase, half):
    odd = lax.axis_index("row") % 2
    return [masks_ref[odd, pl.ds(4 * phase + 2 * half + x, 1), :].astype(BF16) for x in range(2)]


def coded(sums, own, own_re):
    rows, dates = own.shape
    codes = []
    for x in range(2):
        part = sums[:, dates * x:dates * (x + 1)]
        power = jnp.sum(jnp.where(own_re, part, 0.0), axis=0, keepdims=True)
        scale = lax.rsqrt(power + 1e-06)
        own_scale = jnp.sum(jnp.where(own, scale, 0.0), axis=1, keepdims=True)
        codes.append(encode(part * own_scale * scale).reshape(rows // 8, 8, dates))
    return jnp.concatenate(codes, axis=1).astype(BF16)


def message_kernel(samples_ref, far_ref, near_ref):
    rows = samples_ref.shape[0]
    edge = samples_ref[:, LANES:2 * LANES].astype(F32)
    for out_ref, tile, lanes in ((far_ref, 2, 0), (near_ref, 0, 8)):
        out_ref[:rows] = samples_ref[:, LANES * tile:LANES * (tile + 1)]
        parts = [edge[rows // 4 * q:rows // 4 * (q + 1)] for q in range(4)]
        parts = [pltpu.roll(part, LANES - lanes, 1) if lanes else part for part in parts]
        out_ref[rows:] = folded(parts).astype(BF16)


def unfolded(message, lanes):
    rows = message.shape[0] // 5 * 4
    edge = message[rows:].astype(F32)
    turned = [pltpu.roll(edge, (LANES - 8 * q + lanes) % LANES, 1) for q in range(4)]
    return message[:rows], jnp.concatenate(turned, axis=0).astype(BF16)


def own_kernel(samples_ref, masks_ref, sums_ref):
    width = len(OWN_TILES[NEAR]) * LANES
    samples = samples_ref[...]
    view = views(samples)
    for phase in (NEAR, FAR):
        for half in range(2):
            masks = [mask[:, :width] for mask in mask_pair(masks_ref, phase, half)]
            tiles = OWN_TILES[phase]
            sums_ref[2 * phase + half] = products(chosen(samples, tiles), chosen(view, tiles), masks)


def finish_kernel(sums_ref, far_ref, near_ref, masks_ref, out_ref):
    width = len(OWN_TILES[FAR]) * LANES
    rows = near_ref.shape[0] // 5 * 4
    dates = rows // 2
    target, source = iota((rows, dates), 0), iota((rows, dates), 1)
    own = target // 8 * 4 + target % 4 == source
    own_re = own & (target % 8 < 4)
    inner, inner_edge = unfolded(near_ref[...], 8)
    outer, outer_edge = unfolded(far_ref[...], 0)
    halos = jnp.concatenate([inner, inner_edge, outer_edge, outer], axis=1)
    halo_views = views(halos)
    for phase in (NEAR, FAR):
        part = slice(2 * LANES * phase, 2 * LANES * (phase + 1))
        for half in range(2):
            masks = [mask[:, width:] for mask in mask_pair(masks_ref, phase, half)]
            group = 2 * phase + half
            sums = sums_ref[group] + products(halos[:, part], halo_views[:, part], masks)
            out_ref[:, 16 * group:16 * (group + 1), :] = coded(sums, own, own_re)


def spread_kernel(codes_ref, out_ref, codes, results, sems):
    parts = codes_ref.shape[0] // 64
    dates = codes_ref.shape[1]
    odd = lax.axis_index("row") % 2
    codes[...] = codes_ref[...].astype(F32)
    source, target = iota((8 * parts, 8 * parts), 0), iota((8 * parts, 8 * parts), 1)
    cols = 4 * parts
    phase = (target // cols + odd + 1) % 2
    wanted = target % cols // 4 * 8 + phase * 4 + target % 4
    order = (source == wanted).astype(F32).astype(BF16)
    copies = []
    for k in range(8):
        block = codes[pl.ds(k, 8 * parts, stride=8), :].astype(BF16)
        moved = lax.dot_general(block, order, (((0,), (0,)), ((), ())), preferred_element_type=F32)
        moved = decode(moved)
        for y in range(2):
            results[k, pl.ds(y, dates, stride=2), :] = moved[:, cols * y:cols * (y + 1)]
        if k in (3, 6, 7):
            start = {3: 0, 6: 4, 7: 7}[k]
            ready = pl.ds(start, k + 1 - start)
            copies.append(pltpu.make_async_copy(results.at[ready], out_ref.at[ready], sems.at[len(copies)]))
            copies[-1].start()
    for copy in copies:
        copy.wait()


VMEM = pl.BlockSpec(memory_space=pltpu.VMEM)
HBM = pl.BlockSpec(memory_space=pltpu.HBM)


def call(kernel, name, shapes, scratch=(), flops=0, outputs=VMEM):
    def run(*arrays):
        return pl.pallas_call(
            kernel,
            out_shape=[jax.ShapeDtypeStruct(*shape) for shape in shapes],
            in_specs=[VMEM] * len(arrays),
            out_specs=[outputs] * len(shapes),
            scratch_shapes=list(scratch),
            compiler_params=pltpu.CompilerParams(vmem_limit_bytes=32 * 1024 * 1024),
            cost_estimate=pl.CostEstimate(flops=flops, bytes_accessed=1 << 20, transcendentals=0),
            name=name,
        )(*arrays)

    return run


def on_device(slc):
    dates = slc.shape[1]
    rows, cols = slc.shape[2], slc.shape[3]
    groups = lax.axis_size("row")
    parts = lax.axis_size("date")
    total = parts * dates
    width = TILES * LANES
    own = slc.reshape(2 * dates * rows, cols)
    lines = parts * 2 * dates
    chunks = cols // LANES
    (packed,) = call(pack_kernel, "pack", [((lines, width), BF16)])(own)

    def exchange(array):
        blocks = array.reshape(parts, array.size // parts // array.shape[-1], array.shape[-1])
        return lax.all_to_all(blocks, "date", 0, 0, tiled=True).reshape(-1, array.shape[-1])

    def swapped(array, first):
        pairs = [(i, i + 1) for i in range(first, groups - 1, 2)]
        return lax.ppermute(array, "row", pairs + [(j, i) for i, j in pairs])

    samples = exchange(packed)
    far, near = call(
        message_kernel, "message", [((lines // 4 * 5, LANES), BF16)] * 2
    )(samples)
    far, near = swapped(far, 1), swapped(near, 0)
    masks = jnp.asarray(window_masks())
    (sums,) = call(own_kernel, "own", [((4, lines, 2 * total), F32)], flops=1 << 30)(samples, masks)
    (codes,) = call(finish_kernel, "finish", [((parts, 64, total), BF16)], flops=1 << 30)(sums, far, near, masks)
    codes = exchange(codes)
    (out,) = call(
        spread_kernel, "spread", [((2 * dates, 2 * total, chunks * 16), F32)],
        [
            pltpu.VMEM((parts * 64, total), F32),
            pltpu.VMEM((2 * dates, 2 * total, chunks * 16), F32),
            pltpu.SemaphoreType.DMA((dates,)),
        ],
        outputs=HBM,
    )(codes)
    return out.reshape(2, dates, total, rows // 8, cols // 8)


def solution(mesh):
    return jax.shard_map(
        on_device,
        mesh=mesh,
        in_specs=(P(None, "date", "row", None),),
        out_specs=P(None, "date", None, "row", None),
        check_vma=False,
    )
```
